32 devices in a mesh: dp: 8 (over z, x), row: 2 (over core), col: 2 (over y).
Axes of the slice: x: 2, y: 2, z: 4, core: 2. Of those that a mesh axis runs over, the one named last changes fastest.
Arguments:
- tokens: bfloat16 [8192, 768], P(('dp', 'row'), 'col'), may hold values from -6 to 6
- ln1_gain: float32 [768], P('col'), may hold values from 0.25 to 1.75
- ln1_shift: float32 [768], P('col'), may hold values from -3 to 3
- w_qkv: bfloat16 [3, 768, 768], P(None, 'col', 'row'), may hold values from -0.21875 to 0.21875
- qv_bias: float32 [2, 768], P(None, ('row', 'col')), may hold values from -3 to 3
- w_attn_out: bfloat16 [768, 768], P('row', 'col'), may hold values from -0.875 to 0.875
- b_attn_out: float32 [768], P('col'), may hold values from -2 to 2
- ln2_gain: float32 [768], P('col'), may hold values from 0.25 to 1.75
- ln2_shift: float32 [768], P('col'), may hold values from -3 to 3
- w_up: bfloat16 [768, 3072], P('col', 'row'), may hold values from -0.21875 to 0.21875
- b_up: float32 [3072], P(('row', 'col')), may hold values from -3 to 3
- w_down: bfloat16 [3072, 768], P('row', 'col'), may hold values from -0.109375 to 0.109375
- b_down: float32 [768], P('col'), may hold values from -2 to 2
- cotangent: bfloat16 [8192, 768], P(('dp', 'row'), 'col'), may hold values from -12 to 12
Outputs:
- block_out: bfloat16 [8192, 768], P(('dp', 'row'), 'col')
- grad_tokens: bfloat16 [8192, 768], P(('dp', 'row'), 'col')
- grad_ln1_gain: float32 [768], P('col')
- grad_ln1_shift: float32 [768], P('col')
- grad_w_qkv: float32 [3, 768, 768], P(None, 'col', 'row')
- grad_qv_bias: float32 [2, 768], P(None, ('row', 'col'))
- grad_w_attn_out: float32 [768, 768], P('row', 'col')
- grad_b_attn_out: float32 [768], P('col')
- grad_ln2_gain: float32 [768], P('col')
- grad_ln2_shift: float32 [768], P('col')
- grad_w_up: float32 [768, 3072], P('col', 'row')
- grad_b_up: float32 [3072], P(('row', 'col'))
- grad_w_down: float32 [3072, 768], P('row', 'col')
- grad_b_down: float32 [768], P('col')
The draws below stay inside these ranges and needn't reach their ends.
All inputs are finite; a program needn't handle non-finite values.
Results may differ from the reference program's by a relative error of at most 0.011.
Values may be sent and summed in bfloat16 or wider, within the bound.
A program may use at most 128 MiB of HBM per device.

```python
import math
import jax
import jax.numpy as jnp
from jax import lax

D = 768
FF = 3072
HEAD_DIM = 64
SEQLEN = 1024
GROUP = 1024
TOKENS = 8192
N_DP = 8


def draw_cotangent(key, part):
    key = jax.random.fold_in(key, 11)
    position = jnp.arange(TOKENS, dtype=jnp.float32) / TOKENS
    rise = jnp.exp(jnp.log(3.0) * position)[:, None]
    drawn = jax.random.normal(key, (TOKENS, D), jnp.float32) * rise
    return jnp.clip(drawn, -12.0, 12.0).astype(jnp.bfloat16)


def level_of(rng, shape, cuts, low, largest):
    factor_of = 1.0
    for dim, parts in cuts:
        steps = jax.random.uniform(jax.random.fold_in(jax.random.fold_in(rng, 6), dim), (parts,), jnp.float32, low / len(cuts), largest / len(cuts))
        factor_of = factor_of * jnp.repeat(jnp.exp(steps), shape[dim] // parts).reshape((-1,) + (1,) * (len(shape) - 1 - dim))
    return factor_of


def normal_values(own_key, shape, width, limit, cuts=(), held_as=jnp.bfloat16):
    values = jax.random.normal(own_key, shape, jnp.float32) * width
    if len(cuts) > 0:
        values = level_of(own_key, shape, cuts, -0.22, 0.18) * values
    return jnp.clip(values, min=-limit, max=limit).astype(held_as)


def setup_inputs(seed: int = 0) -> dict:
    keys = jax.random.split(jax.random.key(seed), 15)
    return {
        "tokens": normal_values(keys[0], (TOKENS, D), 1.0, 6.0, ((0, 16), (1, 2))),
        "ln1_gain": jnp.clip(1.0 + 0.15 * jax.random.normal(keys[1], (D,), jnp.float32), 0.25, 1.75),
        "ln1_shift": normal_values(keys[2], (D,), 0.5, 3.0, ((0, 2),), jnp.float32),
        "w_qkv": normal_values(keys[3], (3, D, D), D ** -0.5, 0.21875, ((1, 2), (2, 2))),
        "qv_bias": normal_values(keys[4], (2, D), 0.5, 3.0, ((1, 4),), jnp.float32),
        "w_attn_out": normal_values(keys[5], (D, D), (D // 16) ** -0.5, 0.875, ((0, 2), (1, 2))),
        "b_attn_out": normal_values(keys[6], (D,), 0.3, 2.0, ((0, 2),), jnp.float32),
        "ln2_gain": jnp.clip(1.0 + 0.15 * jax.random.normal(keys[7], (D,), jnp.float32), 0.25, 1.75),
        "ln2_shift": normal_values(keys[8], (D,), 0.5, 3.0, ((0, 2),), jnp.float32),
        "w_up": normal_values(keys[9], (D, FF), D ** -0.5, 0.21875, ((0, 2), (1, 2))),
        "b_up": normal_values(keys[10], (FF,), 0.5, 3.0, ((0, 4),), jnp.float32),
        "w_down": normal_values(keys[11], (FF, D), FF ** -0.5, 0.109375, ((0, 2), (1, 2))),
        "b_down": normal_values(keys[12], (D,), 0.3, 2.0, ((0, 2),), jnp.float32),
        "cotangent": draw_cotangent(jax.random.fold_in(keys[14], 71), 0),
    }


@jax.custom_vjp
def low(v):
    return lax.optimization_barrier(v.astype(jnp.bfloat16)).astype(jnp.float32)

@jax.custom_vjp
def low_back(v):
    return v

def low_keep(v):
    return (low(v), None)

def low_pass(kept, grad):
    return (grad,)

def back_keep(v):
    return (v, None)

def back_low(kept, grad):
    return (low(grad),)
low.defvjp(low_keep, low_pass)
low_back.defvjp(back_keep, back_low)
HIGH = lax.Precision.HIGHEST
EPSILON = 1e-05

def layer_norm(values, norm_gain, norm_shift):
    center = lax.optimization_barrier(jnp.mean(values, axis=-1, keepdims=True))
    spread = lax.optimization_barrier(jnp.mean(jnp.square(values - center), axis=-1, keepdims=True))
    return (values - center) * lax.rsqrt(spread + EPSILON) * norm_gain + norm_shift

def attend_block(queries, keys_in, values_in, block_index):
    seq_tokens = keys_in.shape[0]
    block_rows = min(512, seq_tokens)
    first_row = block_index * block_rows
    q_part = lax.dynamic_slice_in_dim(queries, first_row, block_rows, 0)
    score_scale = 1.0 / math.sqrt(HEAD_DIM)
    scores = low_back(jnp.einsum('qhd,khd->hqk', q_part, keys_in, precision=HIGH) * score_scale)
    row_ids = first_row + lax.broadcasted_iota(jnp.int32, (block_rows, seq_tokens), 0)
    col_ids = lax.broadcasted_iota(jnp.int32, (block_rows, seq_tokens), 1)
    scores = jnp.where(col_ids <= row_ids, scores, -1e+30)
    row_max = lax.optimization_barrier(jnp.max(scores, axis=-1, keepdims=True))
    exponent = jnp.exp(scores - row_max)
    probs = exponent / lax.optimization_barrier(jnp.sum(exponent, axis=-1, keepdims=True))
    return jnp.einsum('hqk,khd->qhd', low(probs), values_in, precision=HIGH)

def attention(queries, keys_in, values_in):
    blocks = SEQLEN // min(512, SEQLEN)
    run_block = jax.checkpoint(lambda index: attend_block(queries, keys_in, values_in, index))
    outputs = lax.map(run_block, jnp.arange(blocks, dtype=jnp.int32))
    return outputs.reshape(SEQLEN, -1)

def forward_group(values, params):
    ln1_gain, ln1_shift, w_qkv, qv_bias, w_attn_out, b_attn_out, ln2_gain, ln2_shift, w_up, b_up, w_down, b_down = params
    normed = low(layer_norm(values, ln1_gain, ln1_shift))
    mixed = jnp.einsum('td,jde->jte', normed, w_qkv, precision=HIGH)
    queries = low(low_back(mixed[0] + qv_bias[0]))
    keys_in = low(low_back(mixed[1]))
    values_in = low(low_back(mixed[2] + qv_bias[1]))
    shape_seq = (-1, SEQLEN, D // HEAD_DIM, HEAD_DIM)
    attended = jax.vmap(attention)(queries.reshape(shape_seq), keys_in.reshape(shape_seq), values_in.reshape(shape_seq))
    attended = low(low_back(attended.reshape(values.shape[0], D)))
    hidden_state = values + low_back(jnp.dot(attended, w_attn_out, precision=HIGH) + b_attn_out)
    normed_two = low(layer_norm(hidden_state, ln2_gain, ln2_shift))
    pre_gelu = low_back(jnp.dot(normed_two, w_up, precision=HIGH) + b_up)
    activation = low(jax.nn.gelu(pre_gelu, approximate=False))
    return hidden_state + low_back(jnp.dot(activation, w_down, precision=HIGH) + b_down)

def reference(tokens, ln1_gain, ln1_shift, w_qkv, qv_bias, w_attn_out, b_attn_out, ln2_gain, ln2_shift, w_up, b_up, w_down, b_down, cotangent):
    params = (ln1_gain, ln1_shift, w_qkv.astype(jnp.float32), qv_bias, w_attn_out.astype(jnp.float32), b_attn_out, ln2_gain, ln2_shift, w_up.astype(jnp.float32), b_up, w_down.astype(jnp.float32), b_down)
    groups = tokens.astype(jnp.float32).reshape(N_DP, GROUP, D)
    cot_groups = cotangent.astype(jnp.float32).reshape(N_DP, GROUP, D)

    def scan_step(running, group_items):
        values, cot_group = group_items
        result, pullback = jax.vjp(forward_group, values, params)
        grad_values, grad_params = pullback(cot_group)
        running = tuple((summed + fresh for summed, fresh in zip(running, grad_params)))
        return (running, (result.astype(jnp.bfloat16), grad_values.astype(jnp.bfloat16)))
    initial = tuple((jnp.zeros_like(entry) for entry in params))
    totals, (outputs, grads_in) = lax.scan(scan_step, initial, (groups, cot_groups))
    return (outputs.reshape(TOKENS, D), grads_in.reshape(TOKENS, D), totals[0], totals[1], totals[2], totals[3], totals[4], totals[5], totals[6], totals[7], totals[8], totals[9], totals[10], totals[11])
```

```python
import math

import jax
import jax.numpy as jnp
from jax import lax
from jax.sharding import PartitionSpec as P

D = 768
HEAD_DIM = 64
EPSILON = 1e-05
BF = jnp.bfloat16
F32 = jnp.float32


def swap(x, axis):
    return lax.ppermute(x, axis, [(0, 1), (1, 0)])


def half(x, index, dim):
    size = x.shape[dim] // 2
    return lax.dynamic_slice_in_dim(x, index * size, size, dim)


def ordered(mine, other, index, dim):
    return jnp.where(
        index == 0,
        jnp.concatenate([mine, other], dim),
        jnp.concatenate([other, mine], dim),
    )


def gather_pair(x, axis, index, dim):
    return ordered(x, swap(x, axis), index, dim)


def reduce_pair(x, axis, index, dim):
    sent = half(x, 1 - index, dim).astype(BF)
    return half(x, index, dim) + swap(sent, axis).astype(F32)


def dot(a, b):
    return jnp.dot(a, b, preferred_element_type=F32)


def dot_nt(a, b):
    return lax.dot_general(a, b, (((1,), (1,)), ((), ())), preferred_element_type=F32)


def dot_tn(a, b):
    return lax.dot_general(a, b, (((0,), (0,)), ((), ())), preferred_element_type=F32)


def bit_perm(count, bit):
    return [(i, i ^ (1 << bit)) for i in range(count)]


def group_scatter(x, dim, bits):
    count = lax.axis_size("dp")
    me = lax.axis_index("dp")
    for bit in bits:
        mine = (me >> bit) & 1
        sent = half(x, 1 - mine, dim).astype(BF)
        x = half(x, mine, dim) + lax.ppermute(sent, "dp", bit_perm(count, bit)).astype(F32)
    return x


def group_gather(x, dim, bits):
    count = lax.axis_size("dp")
    me = lax.axis_index("dp")
    x = x.astype(BF)
    for bit in reversed(bits):
        mine = (me >> bit) & 1
        x = ordered(x, lax.ppermute(x, "dp", bit_perm(count, bit)), mine, dim)
    return x.astype(F32)


def norm(values):
    center = jnp.mean(values, axis=1, keepdims=True)
    dev = values - center
    inv = lax.rsqrt(jnp.mean(dev * dev, axis=1, keepdims=True) + EPSILON)
    return dev * inv, inv


def causal_scores(q, k, first):
    s = jnp.einsum("hqd,hkd->hqk", q, k, preferred_element_type=F32) * (1.0 / math.sqrt(HEAD_DIM))
    rows = first + lax.broadcasted_iota(jnp.int32, s.shape[1:], 0)
    cols = lax.broadcasted_iota(jnp.int32, s.shape[1:], 1)
    return jnp.where(cols <= rows, s, -1e30)


def attend(q, k, v):
    seq = q.shape[1]
    block = min(512, seq)
    outs, logs = [], []
    for first in range(0, seq, block):
        last = first + block
        s = causal_scores(q[:, first:last], k[:, :last], first)
        top = jnp.max(s, axis=2, keepdims=True)
        e = jnp.exp(s - top)
        total = jnp.sum(e, axis=2, keepdims=True)
        p = (e / total).astype(BF)
        outs.append(jnp.einsum("hqk,hkd->hqd", p, v[:, :last], preferred_element_type=F32))
        logs.append(top + jnp.log(total))
    return jnp.concatenate(outs, 1), jnp.concatenate(logs, 1)


def attend_back(q, k, v, logs, do):
    seq = q.shape[1]
    block = min(512, seq)
    scale = 1.0 / math.sqrt(HEAD_DIM)
    dk = jnp.zeros(k.shape, F32)
    dv = jnp.zeros(v.shape, F32)
    dq = []
    for first in range(0, seq, block):
        last = first + block
        qp, dop = q[:, first:last], do[:, first:last]
        p = jnp.exp(causal_scores(qp, k[:, :last], first) - logs[:, first:last])
        dp = jnp.einsum("hqd,hkd->hqk", dop, v[:, :last], preferred_element_type=F32)
        ds = (p * (dp - jnp.sum(p * dp, axis=2, keepdims=True))).astype(BF)
        dv = dv.at[:, :last].add(
            jnp.einsum("hqk,hqd->hkd", p.astype(BF), dop, preferred_element_type=F32)
        )
        dq.append(jnp.einsum("hqk,hkd->hqd", ds, k[:, :last], preferred_element_type=F32) * scale)
        dk = dk.at[:, :last].add(
            jnp.einsum("hqk,hqd->hkd", ds, qp, preferred_element_type=F32) * scale
        )
    return jnp.concatenate(dq, 1), dk, dv


def to_heads(x):
    return x.reshape(x.shape[0], -1, HEAD_DIM).swapaxes(0, 1)


def from_heads(x):
    return x.swapaxes(0, 1).reshape(x.shape[1], -1)


def local(
    tokens, ln1_gain, ln1_shift, w_qkv, qv_bias, w_attn_out, b_attn_out,
    ln2_gain, ln2_shift, w_up, b_up, w_down, b_down, cotangent,
):
    r, c = lax.axis_index("row"), lax.axis_index("col")
    nbits = lax.axis_size("dp").bit_length() - 1
    bits_a = list(range(nbits))
    bits_b = [1, 0] + bits_a[2:] if nbits > 1 else bits_a

    vectors = gather_pair(
        jnp.stack([ln1_gain, ln1_shift, ln2_gain, ln2_shift, b_attn_out]), "col", c, 1
    )
    g1, s1, g2, s2, ba = (vectors[i : i + 1] for i in range(5))
    x = gather_pair(tokens, "col", c, 1).astype(F32)
    wq = ordered(half(w_qkv, c, 2), swap(half(w_qkv, 1 - c, 2), "col"), c, 1)
    wa_r = gather_pair(w_attn_out, "col", c, 1)
    wa = gather_pair(wa_r, "row", r, 0)
    wu = ordered(half(w_up, c, 1), swap(half(w_up, 1 - c, 1), "col"), c, 0)
    wd = ordered(half(w_down, c, 0), swap(half(w_down, 1 - c, 0), "col"), c, 1)
    cot_tok = gather_pair(cotangent, "col", c, 1)
    cot = gather_pair(cot_tok, "row", r, 0)

    n1, inv1 = norm(x)
    y1 = gather_pair((n1 * g1 + s1).astype(BF), "row", r, 0)
    q = to_heads((dot(y1, wq[0]) + qv_bias[0]).astype(BF))
    k = to_heads(dot(y1, wq[1]).astype(BF))
    v = to_heads((dot(y1, wq[2]) + qv_bias[1]).astype(BF))
    o, logs = attend(q, k, v)
    o_r = gather_pair(from_heads(o).astype(BF), "col", c, 1)
    o_tok = ordered(half(o_r, r, 0), swap(half(o_r, 1 - r, 0), "row"), r, 1)
    h = x + dot(o_tok, wa) + ba
    n2, inv2 = norm(h)
    y2 = gather_pair((n2 * g2 + s2).astype(BF), "row", r, 0)
    u = dot(y2, wu) + b_up
    phi = 0.5 * (1.0 + lax.erf(u * math.sqrt(0.5)))
    act = (u * phi).astype(BF)
    slope = phi + u * (jnp.exp(-0.5 * u * u) * (1.0 / math.sqrt(2.0 * math.pi)))
    branch = reduce_pair(reduce_pair(dot(act, wd), "row", r, 0), "col", c, 1)
    block_out = (half(h, c, 1) + branch + b_down).astype(BF)

    du32 = dot_nt(cot, wd) * slope
    du = du32.astype(BF)
    dy2 = reduce_pair(dot_nt(du, wu), "row", r, 0)
    dy2 = dy2 + swap(dy2.astype(BF), "col").astype(F32)
    e2 = dy2 * g2
    dhn = inv2 * (
        e2 - jnp.mean(e2, axis=1, keepdims=True) - n2 * jnp.mean(e2 * n2, axis=1, keepdims=True)
    )
    dh = cot_tok.astype(F32) + dhn
    dz_tok = dh.astype(BF)
    dz = gather_pair(dz_tok, "row", r, 0)

    gd = group_scatter(dot_tn(act, cot), 0, bits_a)
    gd = ordered(half(gd, c, 1), swap(half(gd, 1 - c, 1).astype(BF), "col").astype(F32), c, 0)
    gd = group_gather(gd.reshape(2, -1, gd.shape[1]), 1, bits_a).reshape(w_down.shape)

    gu = group_scatter(dot_tn(y2, du).reshape(2, D // 2, -1), 1, bits_b)
    gu = ordered(
        half(gu, c, 0)[0], swap(half(gu, 1 - c, 0)[0].astype(BF), "col").astype(F32), c, 1
    )
    gu = group_gather(gu, 0, bits_b)

    do = to_heads(dot_nt(dz, half(wa_r, c, 0)).astype(BF))
    dq, dk, dv = (from_heads(t).astype(BF) for t in attend_back(q, k, v, logs, do))
    grads_in = [dq, dk, dv]
    dy1 = sum(dot_nt(t, wq[j]) for j, t in enumerate(grads_in))
    dy1 = reduce_pair(dy1, "row", r, 0)
    e1 = dy1 * g1
    sums = jnp.stack([jnp.sum(e1, axis=1), jnp.sum(e1 * n1, axis=1)])
    sums = (sums + swap(sums, "col")) / D
    dy1 = reduce_pair(dy1, "col", c, 1)
    n1c = half(n1, c, 1)
    dxn = inv1 * (dy1 * ln1_gain - sums[0][:, None] - n1c * sums[1][:, None])
    grad_tokens = (half(dh, c, 1) + dxn).astype(BF)

    gq = jnp.stack([dot_tn(y1, t) for t in grads_in]).reshape(3, 2, D // 2, -1)
    gq = group_scatter(gq, 2, bits_a)
    gq = ordered(
        half(gq, c, 1)[:, 0], swap(half(gq, 1 - c, 1)[:, 0].astype(BF), "col").astype(F32), c, 2
    )
    gq = group_gather(gq, 1, bits_a)
    ga = group_gather(group_scatter(dot_tn(o_r, half(dz, c, 1)), 0, bits_b), 0, bits_b)

    def total(t):
        return jnp.sum(t.astype(F32), axis=0)

    dy2c = half(dy2, c, 1)
    by_row = [
        total(dy1 * n1c), total(dy1), total(half(dz_tok, c, 1)),
        total(dy2c * half(n2, c, 1)), total(dy2c), total(cotangent),
    ]
    own = jnp.concatenate([total(dq), total(dv), total(du)])
    zero = jnp.zeros_like(own)
    packed = jnp.concatenate(by_row + [jnp.where(r == 0, own, zero), jnp.where(r == 1, own, zero)])
    packed = lax.psum(packed, ("dp", "row"))
    m = D // 2
    vec = [packed[i * m : (i + 1) * m] for i in range(6)]
    own = half(packed[6 * m :], r, 0)
    f = dq.shape[1]
    gqv = own[: 2 * f].reshape(2, f)
    return (
        block_out, grad_tokens, vec[0], vec[1], gq, gqv, ga, vec[2], vec[3], vec[4],
        gu, own[2 * f :], gd, vec[5],
    )


def solution(mesh):
    placed = (
        P(("dp", "row"), "col"),
        P("col"),
        P("col"),
        P(None, "col", "row"),
        P(None, ("row", "col")),
        P("row", "col"),
        P("col"),
        P("col"),
        P("col"),
        P("col", "row"),
        P(("row", "col")),
        P("row", "col"),
        P("col"),
        P(("dp", "row"), "col"),
    )
    return jax.shard_map(
        local,
        mesh=mesh,
        in_specs=placed,
        out_specs=(
            P(("dp", "row"), "col"),
            P(("dp", "row"), "col"),
            P("col"),
            P("col"),
            P(None, "col", "row"),
            P(None, ("row", "col")),
            P("row", "col"),
            P("col"),
            P("col"),
            P("col"),
            P("col", "row"),
            P(("row", "col")),
            P("row", "col"),
            P("col"),
        ),
        check_vma=False,
    )
```

```python
import math

import jax
import jax.numpy as jnp
from jax import lax
from jax.sharding import PartitionSpec as P

D = 768
HEAD_DIM = 64
EPSILON = 1e-05
BF = jnp.bfloat16
F32 = jnp.float32


def swap(x, axis):
    return lax.ppermute(x, axis, [(0, 1), (1, 0)])


def half(x, index, dim):
    size = x.shape[dim] // 2
    return lax.dynamic_slice_in_dim(x, index * size, size, dim)


def ordered(mine, other, index, dim):
    return jnp.where(
        index == 0,
        jnp.concatenate([mine, other], dim),
        jnp.concatenate([other, mine], dim),
    )


def gather_pair(x, axis, index, dim):
    return ordered(x, swap(x, axis), index, dim)


def reduce_pair(x, axis, index, dim):
    sent = half(x, 1 - index, dim).astype(BF)
    return half(x, index, dim) + swap(sent, axis).astype(F32)


def dot(a, b):
    return jnp.dot(a, b, preferred_element_type=F32)


def dot_nt(a, b):
    return lax.dot_general(a, b, (((1,), (1,)), ((), ())), preferred_element_type=F32)


def dot_tn(a, b):
    return lax.dot_general(a, b, (((0,), (0,)), ((), ())), preferred_element_type=F32)


def bit_perm(count, bit):
    return [(i, i ^ (1 << bit)) for i in range(count)]


def after(x, *earlier):
    pieces = [t.reshape(-1)[:1] if t.ndim == 1 else t[(0,) * (t.ndim - 1)][:1] for t in earlier]
    return lax.optimization_barrier([x] + pieces)[0] if pieces else x


def group_scatter(x, dim, bits, marks=()):
    count = lax.axis_size("dp")
    me = lax.axis_index("dp")
    for step, bit in enumerate(bits):
        mine = (me >> bit) & 1
        sent = half(x, 1 - mine, dim).astype(BF)
        got = after(lax.ppermute(sent, "dp", bit_perm(count, bit)), *marks[step : step + 1])
        x = half(x, mine, dim) + got.astype(F32)
    return x


def group_total(x):
    count = lax.axis_size("dp")
    for bit in range(count.bit_length() - 1):
        x = x + lax.ppermute(x, "dp", bit_perm(count, bit))
    return x


def swap_shared(x, dim):
    count = lax.axis_size("dp")
    if count < 2:
        return swap(x, "col")
    mine = lax.axis_index("dp") & 1
    part = swap(half(x, mine, dim), "col")
    return ordered(part, lax.ppermute(part, "dp", bit_perm(count, 0)), mine, dim)


def group_gather(x, dim, bits):
    count = lax.axis_size("dp")
    me = lax.axis_index("dp")
    x = x.astype(BF)
    for bit in reversed(bits):
        mine = (me >> bit) & 1
        x = ordered(x, lax.ppermute(x, "dp", bit_perm(count, bit)), mine, dim)
    return x.astype(F32)


def norm(values):
    center = jnp.mean(values, axis=1, keepdims=True)
    dev = values - center
    inv = lax.rsqrt(jnp.mean(dev * dev, axis=1, keepdims=True) + EPSILON)
    return dev * inv, inv


def causal_scores(q, k, first):
    s = jnp.einsum("hqd,hkd->hqk", q, k, preferred_element_type=F32) * (1.0 / math.sqrt(HEAD_DIM))
    rows = first + lax.broadcasted_iota(jnp.int32, s.shape[1:], 0)
    cols = lax.broadcasted_iota(jnp.int32, s.shape[1:], 1)
    return jnp.where(cols <= rows, s, -1e30)


def attend(q, k, v):
    seq = q.shape[1]
    block = min(512, seq)
    outs, logs = [], []
    for first in range(0, seq, block):
        last = first + block
        s = causal_scores(q[:, first:last], k[:, :last], first)
        top = jnp.max(s, axis=2, keepdims=True)
        e = jnp.exp(s - top)
        total = jnp.sum(e, axis=2, keepdims=True)
        p = (e / total).astype(BF)
        outs.append(jnp.einsum("hqk,hkd->hqd", p, v[:, :last], preferred_element_type=F32))
        logs.append(top + jnp.log(total))
    return jnp.concatenate(outs, 1), jnp.concatenate(logs, 1)


def attend_back(q, k, v, logs, do):
    seq = q.shape[1]
    block = min(512, seq)
    scale = 1.0 / math.sqrt(HEAD_DIM)
    dk = jnp.zeros(k.shape, F32)
    dv = jnp.zeros(v.shape, F32)
    dq = []
    for first in range(0, seq, block):
        last = first + block
        qp, dop = q[:, first:last], do[:, first:last]
        p = jnp.exp(causal_scores(qp, k[:, :last], first) - logs[:, first:last])
        dp = jnp.einsum("hqd,hkd->hqk", dop, v[:, :last], preferred_element_type=F32)
        ds = (p * (dp - jnp.sum(p * dp, axis=2, keepdims=True))).astype(BF)
        dv = dv.at[:, :last].add(
            jnp.einsum("hqk,hqd->hkd", p.astype(BF), dop, preferred_element_type=F32)
        )
        dq.append(jnp.einsum("hqk,hkd->hqd", ds, k[:, :last], preferred_element_type=F32) * scale)
        dk = dk.at[:, :last].add(
            jnp.einsum("hqk,hqd->hkd", ds, qp, preferred_element_type=F32) * scale
        )
    return dq[0], jnp.concatenate(dq, 1), dk, dv


def to_heads(x):
    return x.reshape(x.shape[0], -1, HEAD_DIM).swapaxes(0, 1)


def from_heads(x):
    return x.swapaxes(0, 1).reshape(x.shape[1], -1)


def local(
    tokens, ln1_gain, ln1_shift, w_qkv, qv_bias, w_attn_out, b_attn_out,
    ln2_gain, ln2_shift, w_up, b_up, w_down, b_down, cotangent,
):
    r, c = lax.axis_index("row"), lax.axis_index("col")
    nbits = lax.axis_size("dp").bit_length() - 1
    bits_a = list(range(nbits))
    bits_b = [1, 0] + bits_a[2:] if nbits > 1 else bits_a

    vectors = gather_pair(
        jnp.stack([ln1_gain, ln1_shift, ln2_gain, ln2_shift, b_attn_out]), "col", c, 1
    )
    g1, s1, g2, s2, ba = (vectors[i : i + 1] for i in range(5))
    wq = ordered(half(w_qkv, c, 2), swap_shared(half(w_qkv, 1 - c, 2), 1), c, 1)
    x_low = gather_pair(tokens, "col", c, 1)
    x = x_low.astype(F32)
    w_attn_out, w_up, w_down, cotangent = (
        after(t, x_low) for t in (w_attn_out, w_up, w_down, cotangent)
    )
    wa_r = ordered(w_attn_out, swap_shared(w_attn_out, 0), c, 1)
    wa = gather_pair(wa_r, "row", r, 0)
    wu = ordered(half(w_up, c, 1), swap_shared(half(w_up, 1 - c, 1), 0), c, 0)
    wd = ordered(half(w_down, c, 0), swap_shared(half(w_down, 1 - c, 0), 0), c, 1)
    cot_tok = gather_pair(cotangent, "col", c, 1)
    cot = gather_pair(cot_tok, "row", r, 0)

    n1, inv1 = norm(x)
    y1 = gather_pair((n1 * g1 + s1).astype(BF), "row", r, 0)
    q = to_heads((dot(y1, wq[0]) + qv_bias[0]).astype(BF))
    k = to_heads(dot(y1, wq[1]).astype(BF))
    v = to_heads((dot(y1, wq[2]) + qv_bias[1]).astype(BF))
    o, logs = attend(q, k, v)
    o_r = gather_pair(from_heads(o).astype(BF), "col", c, 1)
    o_tok = ordered(half(o_r, r, 0), swap(half(o_r, 1 - r, 0), "row"), r, 1)
    h = x + dot(o_tok, wa) + ba
    n2, inv2 = norm(h)
    y2 = gather_pair((n2 * g2 + s2).astype(BF), "row", r, 0)
    u = dot(y2, wu) + b_up
    phi = 0.5 * (1.0 + lax.erf(u * math.sqrt(0.5)))
    act = (u * phi).astype(BF)
    slope = phi + u * (jnp.exp(-0.5 * u * u) * (1.0 / math.sqrt(2.0 * math.pi)))
    branch = reduce_pair(reduce_pair(dot(act, wd), "row", r, 0), "col", c, 1)
    block_out = (half(h, c, 1) + branch + b_down).astype(BF)

    du32 = dot_nt(cot, wd) * slope
    du = du32.astype(BF)
    dy2_part = reduce_pair(dot_nt(du, wu), "row", r, 0)
    dy2 = dy2_part + swap(dy2_part.astype(BF), "col").astype(F32)
    e2 = dy2 * g2
    dhn = inv2 * (
        e2 - jnp.mean(e2, axis=1, keepdims=True) - n2 * jnp.mean(e2 * n2, axis=1, keepdims=True)
    )
    dh = cot_tok.astype(F32) + dhn
    dz_tok = dh.astype(BF)
    dz = gather_pair(dz_tok, "row", r, 0)

    do = to_heads(dot_nt(dz, half(wa_r, c, 0)).astype(BF))
    dq_first, *back = attend_back(q, k, v, logs, do)
    dq, dk, dv = (from_heads(t).astype(BF) for t in back)
    gd = group_scatter(dot_tn(act, cot), 0, bits_a, (dy2_part, dh, do))
    gd = ordered(half(gd, c, 1), swap(half(gd, 1 - c, 1).astype(BF), "col").astype(F32), c, 0)
    gd = group_gather(gd.reshape(2, -1, gd.shape[1]), 1, bits_a).reshape(w_down.shape)

    gu = group_scatter(dot_tn(y2, du).reshape(2, D // 2, -1), 1, bits_b, (do, dq_first, dq))
    gu = ordered(
        half(gu, c, 0)[0], swap(half(gu, 1 - c, 0)[0].astype(BF), "col").astype(F32), c, 1
    )
    gu = group_gather(gu, 0, bits_b)

    grads_in = [dq, dk, dv]
    dy1 = sum(dot_nt(t, wq[j]) for j, t in enumerate(grads_in))
    dy1 = reduce_pair(dy1, "row", r, 0)
    e1 = dy1 * g1
    sums = jnp.stack([jnp.sum(e1, axis=1), jnp.sum(e1 * n1, axis=1)])
    sums = (sums + swap(sums, "col")) / D
    dy1 = reduce_pair(dy1, "col", c, 1)
    n1c = half(n1, c, 1)
    dxn = inv1 * (dy1 * ln1_gain - sums[0][:, None] - n1c * sums[1][:, None])
    grad_tokens = (half(dh, c, 1) + dxn).astype(BF)

    gq = jnp.stack([dot_tn(y1, t) for t in grads_in]).reshape(3, 2, D // 2, -1)
    gq = group_scatter(gq, 2, bits_a)
    gq = ordered(
        half(gq, c, 1)[:, 0], swap(half(gq, 1 - c, 1)[:, 0].astype(BF), "col").astype(F32), c, 2
    )
    gq = group_gather(gq, 1, bits_a)
    ga = group_scatter(dot_tn(o_r, half(dz, c, 1)), 0, bits_b, (dq_first, dq))
    ga = group_gather(ga, 0, bits_b)

    def total(t):
        return jnp.sum(t.astype(F32), axis=0)

    dy2c = half(dy2, c, 1)
    by_row = [
        total(dy1 * n1c), total(dy1), total(half(dz_tok, c, 1)),
        total(dy2c * half(n2, c, 1)), total(dy2c), total(cotangent),
    ]
    by_row = jnp.concatenate(by_row)
    by_row = by_row + swap(by_row, "row")
    own = jnp.concatenate([total(dq), total(dv), total(du)])
    packed = group_total(jnp.concatenate([by_row, own]))
    m = D // 2
    vec = [packed[i * m : (i + 1) * m] for i in range(6)]
    own = packed[6 * m :]
    f = dq.shape[1]
    gqv = own[: 2 * f].reshape(2, f)
    return (
        block_out, grad_tokens, vec[0], vec[1], gq, gqv, ga, vec[2], vec[3], vec[4],
        gu, own[2 * f :], gd, vec[5],
    )


def solution(mesh):
    placed = (
        P(("dp", "row"), "col"),
        P("col"),
        P("col"),
        P(None, "col", "row"),
        P(None, ("row", "col")),
        P("row", "col"),
        P("col"),
        P("col"),
        P("col"),
        P("col", "row"),
        P(("row", "col")),
        P("row", "col"),
        P("col"),
        P(("dp", "row"), "col"),
    )
    return jax.shard_map(
        local,
        mesh=mesh,
        in_specs=placed,
        out_specs=(
            P(("dp", "row"), "col"),
            P(("dp", "row"), "col"),
            P("col"),
            P("col"),
            P(None, "col", "row"),
            P(None, ("row", "col")),
            P("row", "col"),
            P("col"),
            P("col"),
            P("col"),
            P("col", "row"),
            P(("row", "col")),
            P("row", "col"),
            P("col"),
        ),
        check_vma=False,
    )
```

```python
import math

import jax
import jax.numpy as jnp
from jax import lax
from jax.sharding import PartitionSpec as P

D = 768
HEAD_DIM = 64
EPSILON = 1e-05
BF = jnp.bfloat16
F32 = jnp.float32


def swap(x, axis):
    return lax.ppermute(x, axis, [(0, 1), (1, 0)])


def half(x, index, dim):
    size = x.shape[dim] // 2
    return lax.dynamic_slice_in_dim(x, index * size, size, dim)


def ordered(mine, other, index, dim):
    return jnp.where(
        index == 0,
        jnp.concatenate([mine, other], dim),
        jnp.concatenate([other, mine], dim),
    )


def gather_pair(x, axis, index, dim):
    return ordered(x, swap(x, axis), index, dim)


def reduce_pair(x, axis, index, dim):
    sent = half(x, 1 - index, dim).astype(BF)
    return half(x, index, dim) + swap(sent, axis).astype(F32)


def dot(a, b):
    return jnp.dot(a, b, preferred_element_type=F32)


def dot_nt(a, b):
    return lax.dot_general(a, b, (((1,), (1,)), ((), ())), preferred_element_type=F32)


def dot_tn(a, b):
    return lax.dot_general(a, b, (((0,), (0,)), ((), ())), preferred_element_type=F32)


def bit_perm(count, bit):
    return [(i, i ^ (1 << bit)) for i in range(count)]


def after(x, *earlier):
    pieces = [t.reshape(-1)[:1] if t.ndim == 1 else t[(0,) * (t.ndim - 1)][:1] for t in earlier]
    return lax.optimization_barrier([x] + pieces)[0] if pieces else x


def chained(x, *earlier):
    for t in earlier:
        x = x + t[(0,) * t.ndim] * 0.0
    return x


def group_total(x):
    count = lax.axis_size("dp")
    for bit in range(count.bit_length() - 1):
        x = x + lax.ppermute(x, "dp", bit_perm(count, bit))
    return x


def swap_shared(x, dim):
    count = lax.axis_size("dp")
    if count < 2:
        return swap(x, "col")
    mine = lax.axis_index("dp") & 1
    part = swap(half(x, mine, dim), "col")
    return ordered(part, lax.ppermute(part, "dp", bit_perm(count, 0)), mine, dim)


def group_gather(x, dim, bits):
    count = lax.axis_size("dp")
    me = lax.axis_index("dp")
    x = x.astype(BF)
    for bit in reversed(bits):
        mine = (me >> bit) & 1
        x = ordered(x, lax.ppermute(x, "dp", bit_perm(count, bit)), mine, dim)
    return x.astype(F32)


def norm(values):
    center = jnp.mean(values, axis=1, keepdims=True)
    dev = values - center
    inv = lax.rsqrt(jnp.mean(dev * dev, axis=1, keepdims=True) + EPSILON)
    return dev * inv, inv


def causal_scores(q, k, first):
    s = jnp.einsum("hqd,hkd->hqk", q, k, preferred_element_type=F32) * (1.0 / math.sqrt(HEAD_DIM))
    rows = first + lax.broadcasted_iota(jnp.int32, s.shape[1:], 0)
    cols = lax.broadcasted_iota(jnp.int32, s.shape[1:], 1)
    return jnp.where(cols <= rows, s, -1e30)


def attend(q, k, v):
    seq = q.shape[1]
    block = min(512, seq)
    outs, logs = [], []
    for first in range(0, seq, block):
        last = first + block
        s = causal_scores(q[:, first:last], k[:, :last], first)
        top = jnp.max(s, axis=2, keepdims=True)
        e = jnp.exp(s - top)
        total = jnp.sum(e, axis=2, keepdims=True)
        p = (e / total).astype(BF)
        outs.append(jnp.einsum("hqk,hkd->hqd", p, v[:, :last], preferred_element_type=F32))
        logs.append(top + jnp.log(total))
    return jnp.concatenate(outs, 1), jnp.concatenate(logs, 1)


def attend_back(q, k, v, logs, do):
    seq = q.shape[1]
    block = min(512, seq)
    scale = 1.0 / math.sqrt(HEAD_DIM)
    dk = jnp.zeros(k.shape, F32)
    dv = jnp.zeros(v.shape, F32)
    dq = []
    for first in range(0, seq, block):
        last = first + block
        qp, dop = q[:, first:last], do[:, first:last]
        p = jnp.exp(causal_scores(qp, k[:, :last], first) - logs[:, first:last])
        dp = jnp.einsum("hqd,hkd->hqk", dop, v[:, :last], preferred_element_type=F32)
        ds = (p * (dp - jnp.sum(p * dp, axis=2, keepdims=True))).astype(BF)
        dv = dv.at[:, :last].add(
            jnp.einsum("hqk,hqd->hkd", p.astype(BF), dop, preferred_element_type=F32)
        )
        dq.append(jnp.einsum("hqk,hkd->hqd", ds, k[:, :last], preferred_element_type=F32) * scale)
        dk = dk.at[:, :last].add(
            jnp.einsum("hqk,hqd->hkd", ds, qp, preferred_element_type=F32) * scale
        )
    return dq[0], jnp.concatenate(dq, 1), dk, dv


def to_heads(x):
    return x.reshape(x.shape[0], -1, HEAD_DIM).swapaxes(0, 1)


def from_heads(x):
    return x.swapaxes(0, 1).reshape(x.shape[1], -1)


def local(
    tokens, ln1_gain, ln1_shift, w_qkv, qv_bias, w_attn_out, b_attn_out,
    ln2_gain, ln2_shift, w_up, b_up, w_down, b_down, cotangent,
):
    r, c = lax.axis_index("row"), lax.axis_index("col")

    vectors = gather_pair(
        jnp.stack([ln1_gain, ln1_shift, ln2_gain, ln2_shift, b_attn_out]), "col", c, 1
    )
    g1, s1, g2, s2, ba = (vectors[i : i + 1] for i in range(5))
    wq = ordered(half(w_qkv, c, 2), swap(half(w_qkv, 1 - c, 2), "col"), c, 1)
    x_low = gather_pair(tokens, "col", c, 1)
    x = x_low.astype(F32)
    w_attn_out, w_up, w_down, cotangent = (
        after(t, x_low) for t in (w_attn_out, w_up, w_down, cotangent)
    )
    wa_r = ordered(w_attn_out, swap_shared(w_attn_out, 0), c, 1)
    wa = gather_pair(wa_r, "row", r, 0)
    wu = ordered(half(w_up, c, 1), swap_shared(half(w_up, 1 - c, 1), 0), c, 0)
    wd = ordered(half(w_down, c, 0), swap_shared(half(w_down, 1 - c, 0), 0), c, 1)
    cot_tok = gather_pair(cotangent, "col", c, 1)
    cot = gather_pair(cot_tok, "row", r, 0)

    n1, inv1 = norm(x)
    y1 = gather_pair((n1 * g1 + s1).astype(BF), "row", r, 0)
    q = to_heads((dot(y1, wq[0]) + qv_bias[0]).astype(BF))
    k = to_heads(dot(y1, wq[1]).astype(BF))
    v = to_heads((dot(y1, wq[2]) + qv_bias[1]).astype(BF))
    o, logs = attend(q, k, v)
    o_r = gather_pair(from_heads(o).astype(BF), "col", c, 1)
    o_tok = ordered(half(o_r, r, 0), swap(half(o_r, 1 - r, 0), "row"), r, 1)
    h = x + dot(o_tok, wa) + ba
    n2, inv2 = norm(h)
    y2 = gather_pair((n2 * g2 + s2).astype(BF), "row", r, 0)
    u = dot(y2, wu) + b_up
    phi = 0.5 * (1.0 + lax.erf(u * math.sqrt(0.5)))
    act = (u * phi).astype(BF)
    slope = phi + u * (jnp.exp(-0.5 * u * u) * (1.0 / math.sqrt(2.0 * math.pi)))
    branch = reduce_pair(reduce_pair(dot(act, wd), "row", r, 0), "col", c, 1)
    block_out = (half(h, c, 1) + branch + b_down).astype(BF)

    du32 = dot_nt(cot, wd) * slope
    du = du32.astype(BF)
    dy2_part = reduce_pair(dot_nt(du, wu), "row", r, 0)
    dy2 = dy2_part + swap(dy2_part.astype(BF), "col").astype(F32)
    e2 = dy2 * g2
    dhn = inv2 * (
        e2 - jnp.mean(e2, axis=1, keepdims=True) - n2 * jnp.mean(e2 * n2, axis=1, keepdims=True)
    )
    dh = cot_tok.astype(F32) + dhn
    dz_tok = dh.astype(BF)
    dz = gather_pair(dz_tok, "row", r, 0)

    do = to_heads(dot_nt(dz, half(wa_r, c, 0)).astype(BF))
    dq_first, *back = attend_back(q, k, v, logs, do)
    dq, dk, dv = (from_heads(t).astype(BF) for t in back)
    gd = dot_tn(act, cot).astype(BF)
    gd = ordered(half(gd, c, 1), swap(half(gd, 1 - c, 1), "col"), c, 0)
    gd = lax.psum(gd, "dp")
    gu = dot_tn(y2, du).astype(BF)
    gu = ordered(half(gu, c, 0), swap(after(half(gu, 1 - c, 0), dh), "col"), c, 1)
    ga = dot_tn(o_r, half(dz, c, 1)).astype(BF)
    gu, ga = lax.psum((chained(gu, gd), ga), "dp")
    grads_in = [dq, dk, dv]
    dy1 = sum(dot_nt(t, wq[j]) for j, t in enumerate(grads_in))
    dy1 = reduce_pair(dy1, "row", r, 0)
    e1 = dy1 * g1
    sums = jnp.stack([jnp.sum(e1, axis=1), jnp.sum(e1 * n1, axis=1)])
    sums = (sums + swap(sums, "col")) / D
    dy1 = reduce_pair(dy1, "col", c, 1)
    n1c = half(n1, c, 1)
    dxn = inv1 * (dy1 * ln1_gain - sums[0][:, None] - n1c * sums[1][:, None])
    grad_tokens = (half(dh, c, 1) + dxn).astype(BF)

    gq = jnp.stack([dot_tn(y1, t) for t in grads_in]).astype(BF)
    gq = ordered(half(gq, c, 1), swap(half(gq, 1 - c, 1), "col"), c, 2)
    gq = lax.psum(chained(gq, gu), "dp").astype(F32)
    gd, gu, ga = (t.astype(F32) for t in (gd, gu, ga))

    def total(t):
        return jnp.sum(t.astype(F32), axis=0)

    dy2c = half(dy2, c, 1)
    by_row = [
        total(dy1 * n1c), total(dy1), total(half(dz_tok, c, 1)),
        total(dy2c * half(n2, c, 1)), total(dy2c), total(cotangent),
    ]
    by_row = jnp.concatenate(by_row)
    by_row = by_row + swap(by_row, "row")
    own = jnp.concatenate([total(dq), total(dv), total(du)])
    packed = group_total(jnp.concatenate([by_row, own]))
    m = D // 2
    vec = [packed[i * m : (i + 1) * m] for i in range(6)]
    own = packed[6 * m :]
    f = dq.shape[1]
    gqv = own[: 2 * f].reshape(2, f)
    return (
        block_out, grad_tokens, vec[0], vec[1], gq, gqv, ga, vec[2], vec[3], vec[4],
        gu, own[2 * f :], gd, vec[5],
    )


def solution(mesh):
    placed = (
        P(("dp", "row"), "col"),
        P("col"),
        P("col"),
        P(None, "col", "row"),
        P(None, ("row", "col")),
        P("row", "col"),
        P("col"),
        P("col"),
        P("col"),
        P("col", "row"),
        P(("row", "col")),
        P("row", "col"),
        P("col"),
        P(("dp", "row"), "col"),
    )
    return jax.shard_map(
        local,
        mesh=mesh,
        in_specs=placed,
        out_specs=(
            P(("dp", "row"), "col"),
            P(("dp", "row"), "col"),
            P("col"),
            P("col"),
            P(None, "col", "row"),
            P(None, ("row", "col")),
            P("row", "col"),
            P("col"),
            P("col"),
            P("col"),
            P("col", "row"),
            P(("row", "col")),
            P("row", "col"),
            P("col"),
        ),
        check_vma=False,
    )
```

```python
import math

import jax
import jax.numpy as jnp
from jax import lax
from jax.sharding import PartitionSpec as P

D = 768
HEAD_DIM = 64
EPSILON = 1e-05
BF = jnp.bfloat16
F32 = jnp.float32


def swap(x, axis):
    return lax.ppermute(x, axis, [(0, 1), (1, 0)])


def half(x, index, dim):
    size = x.shape[dim] // 2
    return lax.dynamic_slice_in_dim(x, index * size, size, dim)


def ordered(mine, other, index, dim):
    return jnp.where(
        index == 0,
        jnp.concatenate([mine, other], dim),
        jnp.concatenate([other, mine], dim),
    )


def gather_pair(x, axis, index, dim):
    return ordered(x, swap(x, axis), index, dim)


def reduce_pair(x, axis, index, dim):
    sent = half(x, 1 - index, dim).astype(BF)
    return half(x, index, dim) + swap(sent, axis).astype(F32)


def dot(a, b):
    return jnp.dot(a, b, preferred_element_type=F32)


def dot_nt(a, b):
    return lax.dot_general(a, b, (((1,), (1,)), ((), ())), preferred_element_type=F32)


def dot_tn(a, b):
    return lax.dot_general(a, b, (((0,), (0,)), ((), ())), preferred_element_type=F32)


def bit_perm(count, bit):
    return [(i, i ^ (1 << bit)) for i in range(count)]


def after(x, *earlier):
    pieces = [t.reshape(-1)[:1] if t.ndim == 1 else t[(0,) * (t.ndim - 1)][:1] for t in earlier]
    return lax.optimization_barrier([x] + pieces)[0] if pieces else x


def group_scatter(x, dim, bits, marks=()):
    count = lax.axis_size("dp")
    me = lax.axis_index("dp")
    for step, bit in enumerate(bits):
        mine = (me >> bit) & 1
        sent = half(x, 1 - mine, dim).astype(BF)
        got = after(lax.ppermute(sent, "dp", bit_perm(count, bit)), *marks[step : step + 1])
        x = half(x, mine, dim) + got.astype(F32)
    return x


def group_total(x):
    count = lax.axis_size("dp")
    for bit in range(count.bit_length() - 1):
        x = x + lax.ppermute(x, "dp", bit_perm(count, bit))
    return x


def swap_shared(x, dim):
    count = lax.axis_size("dp")
    if count < 2:
        return swap(x, "col")
    mine = lax.axis_index("dp") & 1
    part = swap(half(x, mine, dim), "col")
    return ordered(part, lax.ppermute(part, "dp", bit_perm(count, 0)), mine, dim)


def group_gather(x, dim, bits):
    count = lax.axis_size("dp")
    me = lax.axis_index("dp")
    x = x.astype(BF)
    for bit in reversed(bits):
        mine = (me >> bit) & 1
        x = ordered(x, lax.ppermute(x, "dp", bit_perm(count, bit)), mine, dim)
    return x.astype(F32)


def norm(values):
    center = jnp.mean(values, axis=1, keepdims=True)
    dev = values - center
    inv = lax.rsqrt(jnp.mean(dev * dev, axis=1, keepdims=True) + EPSILON)
    return dev * inv, inv


def causal_scores(q, k, first):
    s = jnp.einsum("hqd,hkd->hqk", q, k, preferred_element_type=F32) * (1.0 / math.sqrt(HEAD_DIM))
    rows = first + lax.broadcasted_iota(jnp.int32, s.shape[1:], 0)
    cols = lax.broadcasted_iota(jnp.int32, s.shape[1:], 1)
    return jnp.where(cols <= rows, s, -1e30)


def attend(q, k, v):
    seq = q.shape[1]
    block = min(512, seq)
    outs, logs = [], []
    for first in range(0, seq, block):
        last = first + block
        s = causal_scores(q[:, first:last], k[:, :last], first)
        top = jnp.max(s, axis=2, keepdims=True)
        e = jnp.exp(s - top)
        total = jnp.sum(e, axis=2, keepdims=True)
        p = (e / total).astype(BF)
        outs.append(jnp.einsum("hqk,hkd->hqd", p, v[:, :last], preferred_element_type=F32))
        logs.append(top + jnp.log(total))
    return jnp.concatenate(outs, 1), jnp.concatenate(logs, 1)


def attend_back(q, k, v, logs, do):
    seq = q.shape[1]
    block = min(512, seq)
    scale = 1.0 / math.sqrt(HEAD_DIM)
    dk = jnp.zeros(k.shape, F32)
    dv = jnp.zeros(v.shape, F32)
    dq = []
    for first in range(0, seq, block):
        last = first + block
        qp, dop = q[:, first:last], do[:, first:last]
        p = jnp.exp(causal_scores(qp, k[:, :last], first) - logs[:, first:last])
        dp = jnp.einsum("hqd,hkd->hqk", dop, v[:, :last], preferred_element_type=F32)
        ds = (p * (dp - jnp.sum(p * dp, axis=2, keepdims=True))).astype(BF)
        dv = dv.at[:, :last].add(
            jnp.einsum("hqk,hqd->hkd", p.astype(BF), dop, preferred_element_type=F32)
        )
        dq.append(jnp.einsum("hqk,hkd->hqd", ds, k[:, :last], preferred_element_type=F32) * scale)
        dk = dk.at[:, :last].add(
            jnp.einsum("hqk,hqd->hkd", ds, qp, preferred_element_type=F32) * scale
        )
    return dq[0], jnp.concatenate(dq, 1), dk, dv


def to_heads(x):
    return x.reshape(x.shape[0], -1, HEAD_DIM).swapaxes(0, 1)


def from_heads(x):
    return x.swapaxes(0, 1).reshape(x.shape[1], -1)


def local(
    tokens, ln1_gain, ln1_shift, w_qkv, qv_bias, w_attn_out, b_attn_out,
    ln2_gain, ln2_shift, w_up, b_up, w_down, b_down, cotangent,
):
    r, c = lax.axis_index("row"), lax.axis_index("col")
    nbits = lax.axis_size("dp").bit_length() - 1
    bits_a = list(range(nbits))
    bits_b = [1, 0] + bits_a[2:] if nbits > 1 else bits_a

    vectors = gather_pair(
        jnp.stack([ln1_gain, ln1_shift, ln2_gain, ln2_shift, b_attn_out]), "col", c, 1
    )
    g1, s1, g2, s2, ba = (vectors[i : i + 1] for i in range(5))
    wq = ordered(half(w_qkv, c, 2), swap(half(w_qkv, 1 - c, 2), "col"), c, 1)
    x_low = gather_pair(tokens, "col", c, 1)
    x = x_low.astype(F32)
    w_attn_out, w_up, w_down, cotangent = (
        after(t, x_low) for t in (w_attn_out, w_up, w_down, cotangent)
    )
    wa_r = ordered(w_attn_out, swap_shared(w_attn_out, 0), c, 1)
    wa = gather_pair(wa_r, "row", r, 0)
    wu = ordered(half(w_up, c, 1), swap_shared(half(w_up, 1 - c, 1), 0), c, 0)
    wd = ordered(half(w_down, c, 0), swap_shared(half(w_down, 1 - c, 0), 0), c, 1)
    cot_tok = gather_pair(cotangent, "col", c, 1)
    cot = gather_pair(cot_tok, "row", r, 0)

    n1, inv1 = norm(x)
    y1 = gather_pair((n1 * g1 + s1).astype(BF), "row", r, 0)
    q = to_heads((dot(y1, wq[0]) + qv_bias[0]).astype(BF))
    k = to_heads(dot(y1, wq[1]).astype(BF))
    v = to_heads((dot(y1, wq[2]) + qv_bias[1]).astype(BF))
    o, logs = attend(q, k, v)
    o_r = gather_pair(from_heads(o).astype(BF), "col", c, 1)
    o_tok = ordered(half(o_r, r, 0), swap(half(o_r, 1 - r, 0), "row"), r, 1)
    h = x + dot(o_tok, wa) + ba
    n2, inv2 = norm(h)
    y2 = gather_pair((n2 * g2 + s2).astype(BF), "row", r, 0)
    u = dot(y2, wu) + b_up
    phi = 0.5 * (1.0 + lax.erf(u * math.sqrt(0.5)))
    act = (u * phi).astype(BF)
    slope = phi + u * (jnp.exp(-0.5 * u * u) * (1.0 / math.sqrt(2.0 * math.pi)))
    branch = reduce_pair(reduce_pair(dot(act, wd), "row", r, 0), "col", c, 1)
    block_out = (half(h, c, 1) + branch + b_down).astype(BF)

    du32 = dot_nt(cot, wd) * slope
    du = du32.astype(BF)
    dy2_part = reduce_pair(dot_nt(du, wu), "row", r, 0)
    dy2 = dy2_part + swap(dy2_part.astype(BF), "col").astype(F32)
    e2 = dy2 * g2
    dhn = inv2 * (
        e2 - jnp.mean(e2, axis=1, keepdims=True) - n2 * jnp.mean(e2 * n2, axis=1, keepdims=True)
    )
    dh = cot_tok.astype(F32) + dhn
    dz_tok = dh.astype(BF)
    dz = gather_pair(dz_tok, "row", r, 0)

    do = to_heads(dot_nt(dz, half(wa_r, c, 0)).astype(BF))
    dq_first, *back = attend_back(q, k, v, logs, do)
    dq, dk, dv = (from_heads(t).astype(BF) for t in back)
    gd = group_scatter(dot_tn(act, cot), 0, bits_a, (dy2_part, dh, do))
    gd = ordered(half(gd, c, 1), swap(half(gd, 1 - c, 1).astype(BF), "col").astype(F32), c, 0)
    gd = group_gather(gd.reshape(2, -1, gd.shape[1]), 1, bits_a).reshape(w_down.shape)

    gu = group_scatter(dot_tn(y2, du).reshape(2, D // 2, -1), 1, bits_b, (do, dq_first, dq))
    gu = ordered(
        half(gu, c, 0)[0], swap(half(gu, 1 - c, 0)[0].astype(BF), "col").astype(F32), c, 1
    )
    gu = group_gather(gu, 0, bits_b)

    grads_in = [dq, dk, dv]
    dy1 = sum(dot_nt(t, wq[j]) for j, t in enumerate(grads_in))
    dy1 = reduce_pair(dy1, "row", r, 0)
    e1 = dy1 * g1
    sums = jnp.stack([jnp.sum(e1, axis=1), jnp.sum(e1 * n1, axis=1)])
    sums = (sums + swap(sums, "col")) / D
    dy1 = reduce_pair(dy1, "col", c, 1)
    n1c = half(n1, c, 1)
    dxn = inv1 * (dy1 * ln1_gain - sums[0][:, None] - n1c * sums[1][:, None])
    grad_tokens = (half(dh, c, 1) + dxn).astype(BF)

    ga = dot_tn(o_r, half(dz, c, 1))
    ga = jnp.stack(jnp.split(ga, 2, axis=1))
    gq = jnp.stack([dot_tn(y1, t).reshape(2, D // 2, -1) for t in grads_in] + [ga])
    gq = group_scatter(gq, 2, bits_a)
    ga = jnp.concatenate([gq[3, 0], gq[3, 1]], axis=1)
    gq = gq[:3]
    gq = ordered(
        half(gq, c, 1)[:, 0], swap(half(gq, 1 - c, 1)[:, 0].astype(BF), "col").astype(F32), c, 2
    )
    gq = group_gather(jnp.concatenate([gq, ga[None]]), 1, bits_a)
    gq, ga = gq[:3], gq[3]

    def total(t):
        return jnp.sum(t.astype(F32), axis=0)

    dy2c = half(dy2, c, 1)
    by_row = [
        total(dy1 * n1c), total(dy1), total(half(dz_tok, c, 1)),
        total(dy2c * half(n2, c, 1)), total(dy2c), total(cotangent),
    ]
    by_row = jnp.concatenate(by_row)
    by_row = by_row + swap(by_row, "row")
    own = jnp.concatenate([total(dq), total(dv), total(du)])
    packed = group_total(jnp.concatenate([by_row, own]))
    m = D // 2
    vec = [packed[i * m : (i + 1) * m] for i in range(6)]
    own = packed[6 * m :]
    f = dq.shape[1]
    gqv = own[: 2 * f].reshape(2, f)
    return (
        block_out, grad_tokens, vec[0], vec[1], gq, gqv, ga, vec[2], vec[3], vec[4],
        gu, own[2 * f :], gd, vec[5],
    )


def solution(mesh):
    placed = (
        P(("dp", "row"), "col"),
        P("col"),
        P("col"),
        P(None, "col", "row"),
        P(None, ("row", "col")),
        P("row", "col"),
        P("col"),
        P("col"),
        P("col"),
        P("col", "row"),
        P(("row", "col")),
        P("row", "col"),
        P("col"),
        P(("dp", "row"), "col"),
    )
    return jax.shard_map(
        local,
        mesh=mesh,
        in_specs=placed,
        out_specs=(
            P(("dp", "row"), "col"),
            P(("dp", "row"), "col"),
            P("col"),
            P("col"),
            P(None, "col", "row"),
            P(None, ("row", "col")),
            P("row", "col"),
            P("col"),
            P("col"),
            P("col"),
            P("col", "row"),
            P(("row", "col")),
            P("row", "col"),
            P("col"),
        ),
        check_vma=False,
    )
```
